32 devices in a mesh: example: 4 (over x, core), seq: 8 (over z, y).
Axes of the slice: x: 2, y: 2, z: 4, core: 2. Of those that a mesh axis runs over, the one named last changes fastest.
Arguments:
- activations: bfloat16 [4, 2048, 4096], P('example', 'seq'), may hold values from -6 to 6
- gate_weight: bfloat16 [4096, 256], P('seq'), may hold values from -0.09375 to 0.09375
- seeds: bfloat16 [4, 2048, 256], P('example', 'seq'), may hold values from -6 to 6
Outputs:
- fisher: float32 [4096, 256], P('seq', 'example')
The draws below stay inside these ranges and needn't reach their ends.
All inputs are finite; a program needn't handle non-finite values.
Results may differ from the reference program's by a relative error of at most 0.0024.
Values may be sent and summed in bfloat16 or wider, within the bound.
No kernel may reach another device: no remote copies, remote signals or barrier semaphores. Data moves between devices by JAX's collectives and lax.ppermute only.
A program may use at most 64 MiB of HBM per device.

```python
import jax
import jax.numpy as jnp
from jax import lax

D = 4096
F = 256
SEQ_LEN = 2048
EXAMPLES = 4


def raised(entries, key, source, target, blocks, factor):
    def block_of(dim):
        return (jnp.arange(entries.shape[dim]) // (entries.shape[dim] // blocks)).reshape((-1,) + (1,) * (entries.ndim - 1 - dim))

    first = jax.random.permutation(key, blocks)[block_of(target)]
    second = (block_of(target) + blocks // 2) % blocks
    return jnp.where((block_of(source) == first) | (block_of(source) == second), factor * entries, entries)


def block_levels(key, shape, shards, smallest, top_value):
    factor_of = 1.0
    for position, blocks in shards:
        heights = jax.random.uniform(jax.random.fold_in(jax.random.fold_in(key, 6), position), (blocks,), jnp.float32, smallest / len(shards), top_value / len(shards))
        factor_of = factor_of * jnp.repeat(jnp.exp(heights), shape[position] // blocks).reshape((-1,) + (1,) * (len(shape) - 1 - position))
    return factor_of


def bell_draw(stream_key, dims, scale, limit, cuts=(), held_as=jnp.bfloat16):
    drawn = jax.random.normal(stream_key, dims, jnp.float32) * scale
    if len(cuts) > 0:
        drawn = block_levels(stream_key, dims, cuts, -0.22, 0.18) * drawn
    return jnp.clip(drawn, min=-limit, max=limit).astype(held_as)


def bell_draw_with(own_key, dims, width, reach, split, heavy, held_as=jnp.bfloat16):
    entries = width * jax.random.normal(own_key, dims, jnp.float32)
    if split:
        entries = entries * block_levels(own_key, dims, split, -0.22, 0.18)
    return jnp.clip(raised(entries, jax.random.fold_in(own_key, 3), *heavy), -reach, reach).astype(held_as)


def setup_inputs(seed: int = 0) -> dict:
    key_list = jax.random.split(jax.random.key(seed), 4)
    activations = bell_draw_with(key_list[0], (EXAMPLES, SEQ_LEN, D), 1.0, 6.0, ((0, 4), (1, 8)), (1, 2, 8, 2.0))
    gate_weight = bell_draw(key_list[1], (D, F), D ** -0.5, 0.09375, ((0, 8),))
    seeds = bell_draw(key_list[2], (EXAMPLES, SEQ_LEN, F), 1.0, 6.0, ((0, 4), (1, 8)))
    return dict(activations=activations, gate_weight=gate_weight, seeds=seeds)


def one_example(pair, gate_weight):
    inputs, cotangent = pair
    pre = jnp.dot(inputs, gate_weight, preferred_element_type=jnp.float32)
    sigma = jax.nn.sigmoid(pre)
    local = (cotangent.astype(jnp.float32) * sigma * (1.0 + pre * (1.0 - sigma))).astype(jnp.bfloat16)
    grad = lax.dot_general(inputs, local, (((0,), (0,)), ((), ())), preferred_element_type=jnp.float32)
    grad = grad / jnp.sqrt(jnp.float32(SEQ_LEN))
    return grad * grad

def reference(activations, gate_weight, seeds):
    squares = lax.map(lambda pair: one_example(pair, gate_weight), (activations, seeds))
    return lax.optimization_barrier(jnp.sum(squares, axis=0)) / jnp.float32(EXAMPLES)
```

```python
import functools

import jax
import jax.numpy as jnp
from jax import lax
from jax.experimental import pallas as pl
from jax.experimental.pallas import tpu as pltpu
from jax.sharding import PartitionSpec as P

F32 = jnp.float32
BF16 = jnp.bfloat16


def local_terms(cotangent, pre):
    sigma = jax.nn.sigmoid(pre)
    return (cotangent.astype(F32) * sigma * (1.0 + pre * (1.0 - sigma))).astype(BF16)


def hop(x, axis, k):
    return lax.ppermute(x, axis, [(i, i ^ k) for i in range(lax.axis_size(axis))])


def columns(block, size):
    return pl.ds(pl.multiple_of(block * size, 128), size)


def call(kernel, outs, flops, *operands):
    vmem = pl.BlockSpec(memory_space=pltpu.VMEM)
    moved = sum(x.size * x.dtype.itemsize for x in (*operands, *outs))
    return pl.pallas_call(
        kernel,
        out_shape=tuple(outs),
        in_specs=[vmem] * len(operands),
        out_specs=(vmem,) * len(outs),
        compiler_params=pltpu.CompilerParams(vmem_limit_bytes=48 * 2**20),
        cost_estimate=pl.CostEstimate(flops=flops, bytes_accessed=moved, transcendentals=0),
    )(*operands)


def local_kernel(rows, *refs):
    a, seeds, own, *pieces = refs[:-2]
    local_ref, first = refs[-2:]
    half = rows // 2
    me = lax.axis_index("seq")
    core = lax.rem(lax.axis_index("example"), 2)
    pre = jnp.dot(a[:, columns(me, rows)], own[...], preferred_element_type=F32)
    count = lax.axis_size("seq")
    for k in range(1, count):
        for flip in range(2):
            block = 2 * (me ^ k) + (core ^ flip)
            pre += jnp.dot(
                a[:, columns(block, half)], pieces[2 * (k - 1) + flip][...], preferred_element_type=F32
            )
    local_t = local_terms(seeds[...], pre).T
    local_ref[...] = local_t
    k = count - 1
    first[...] = jnp.dot(
        local_t, a[:, columns(me ^ k, rows)], preferred_element_type=F32
    ).astype(first.dtype)


def product_kernel(rows, blocks, a, local_t, *outs):
    me = lax.axis_index("seq")
    for k, out in zip(blocks, outs):
        out[...] = jnp.dot(
            local_t[...], a[:, columns(me ^ k, rows)], preferred_element_type=F32
        ).astype(out.dtype)


def add_kernel(mine, other, out):
    out[...] = (mine[...] + other[...].astype(F32)).astype(out.dtype)


def square_kernel(mine, *refs):
    examples = lax.axis_size("example")
    arrived, outs = refs[: len(refs) - examples], refs[len(refs) - examples :]
    me = lax.axis_index("example")
    size = outs[0].shape[0]
    for k, out in enumerate(outs):
        part = pl.ds(pl.multiple_of((me ^ k) * size, size), size)
        grad = mine[part, :]
        for other in arrived:
            grad += other[part, :].astype(F32)
        out[...] = (grad * grad).astype(out.dtype)


def mean_kernel(scale, own, *refs):
    total = own[...]
    for other in refs[:-1]:
        total += other[...].astype(F32)
    refs[-1][...] = total * scale


def direct(activations, gate_weight, seeds):
    inputs, cotangent = activations[0], seeds[0]
    tokens, width = inputs.shape
    rows, hidden = gate_weight.shape
    count, examples = lax.axis_size("seq"), lax.axis_size("example")
    core = lax.rem(lax.axis_index("example"), 2)
    lines = count // 2

    half = lax.dynamic_slice_in_dim(gate_weight, core * (rows // 2), rows // 2)
    held = {0: half}
    for k in range(1, lines):
        held[2 * k] = hop(half, "seq", 2 * k)
    for k in range(lines):
        held[2 * k + 1] = hop(held[2 * k], "seq", 1)
    pieces = []
    for k in range(1, count):
        pieces += [held[k], hop(held[k], "example", 1)]

    dots = 2 * tokens * hidden
    block = lambda dtype: jax.ShapeDtypeStruct((hidden, rows), dtype)
    local_t, first = call(
        functools.partial(local_kernel, rows),
        (jax.ShapeDtypeStruct((hidden, tokens), BF16), block(BF16)),
        dots * (width + rows),
        inputs, cotangent, gate_weight, *pieces,
    )
    order = [2 * k for k in reversed(range(lines))]
    sent = {order[0]: first}
    later = [k + 1 for k in order[1:]] + order
    made = call(
        functools.partial(product_kernel, rows, later),
        [block(BF16)] * (lines - 1) + [block(F32)] * lines,
        dots * rows * len(later),
        inputs, local_t,
    )
    sent.update(zip(order[1:], made))
    mine = dict(zip(order, made[lines - 1 :]))

    arrived = []
    for k in order:
        other = hop(sent[k], "seq", 1)
        if k:
            (pair,) = call(add_kernel, (block(BF16),), mine[k].size, mine[k], other)
            arrived.append(hop(pair, "seq", k))
        else:
            arrived.append(other)

    size = hidden // examples
    part = lambda dtype: jax.ShapeDtypeStruct((size, rows), dtype)
    own, *others = call(
        square_kernel, [part(F32)] + [part(BF16)] * (examples - 1), 8 * hidden * rows, mine[0], *arrived
    )
    others = [hop(x, "example", k + 1) for k, x in enumerate(others)]
    (total,) = call(
        functools.partial(mean_kernel, 1.0 / (tokens * count * examples)),
        (part(F32),), 4 * size * rows, own, *others,
    )
    return total.T


def plain(activations, gate_weight, seeds):
    inputs, cotangent = activations[0], seeds[0]
    count, examples = lax.axis_size("seq"), lax.axis_size("example")
    weights = lax.all_gather(gate_weight, "seq", axis=0, tiled=True)
    pre = jnp.dot(inputs, weights, preferred_element_type=F32)
    local = local_terms(cotangent, pre)
    product = lax.dot_general(inputs, local, (((0,), (0,)), ((), ())), preferred_element_type=F32)
    grad = lax.psum_scatter(product, "seq", scatter_dimension=0, tiled=True)
    total = lax.psum_scatter(grad * grad, "example", scatter_dimension=1, tiled=True)
    return total * (1.0 / (inputs.shape[0] * count * examples))


def body(activations, gate_weight, seeds):
    rows, hidden = gate_weight.shape
    aligned = rows % 256 == 0 and (hidden // lax.axis_size("example")) % 16 == 0
    return (direct if aligned else plain)(activations, gate_weight, seeds)


def solution(mesh):
    return jax.shard_map(
        body,
        mesh=mesh,
        in_specs=(P("example", "seq", None), P("seq", None), P("example", "seq", None)),
        out_specs=P("seq", "example"),
        check_vma=False,
    )
```

```python
import functools

import jax
import jax.numpy as jnp
from jax import lax
from jax.experimental import pallas as pl
from jax.experimental.pallas import tpu as pltpu
from jax.sharding import PartitionSpec as P

COST = 20_000_000_000
F32 = jnp.float32
BF16 = jnp.bfloat16


def local_terms(cotangent, pre):
    sigma = jax.nn.sigmoid(pre)
    return (cotangent.astype(F32) * sigma * (1.0 + pre * (1.0 - sigma))).astype(BF16)


def hop(x, axis, k):
    return lax.ppermute(x, axis, [(i, i ^ k) for i in range(lax.axis_size(axis))])


def move(x, axis, hops):
    return lax.ppermute(x, axis, [(i, i ^ k) for i, k in hops.items()])


def columns(block, size):
    return pl.ds(pl.multiple_of(block * size, 128), size)


def call(kernel, outs, *operands, cost=COST):
    vmem = pl.BlockSpec(memory_space=pltpu.VMEM)
    moved = sum(x.size * x.dtype.itemsize for x in (*operands, *outs))
    return pl.pallas_call(
        kernel,
        out_shape=tuple(outs),
        in_specs=[vmem] * len(operands),
        out_specs=(vmem,) * len(outs),
        compiler_params=pltpu.CompilerParams(vmem_limit_bytes=48 * 2**20),
        cost_estimate=pl.CostEstimate(flops=cost, bytes_accessed=moved, transcendentals=0),
    )(*operands)


def encode(x):
    return (x * jnp.abs(x)).astype(BF16)


def decode(y):
    y = y.astype(F32)
    root = jnp.sqrt(jnp.abs(y))
    return jnp.where(y < 0, -root, root)


def put(out, value):
    out[...] = encode(value) if out.dtype == BF16 else value


def add_pieces(pre, a, hops, pieces):
    half = pieces[0].shape[0]
    me = lax.axis_index("seq")
    core = lax.rem(lax.axis_index("example"), 2)
    for i, k in enumerate(hops):
        for flip in range(2):
            block = 2 * (me ^ k) + (core ^ flip)
            pre += jnp.dot(
                a[:, columns(block, half)], pieces[2 * i + flip][...], preferred_element_type=F32
            )
    return pre


def chunk(hops, a, local_t):
    rows = a.shape[1] // lax.axis_size("seq")
    block = lax.axis_index("seq") ^ hops
    return jnp.dot(local_t, a[:, columns(block, rows)], preferred_element_type=F32)


def pass_kernel(piece, out):
    out[...] = piece[...]


def local_kernel(hops, send, a, seeds, own, *refs):
    count = len(refs) - len(send) - 1
    pieces, outs, local_ref = refs[:count], refs[count:-1], refs[-1]
    block = a[:, columns(lax.axis_index("seq"), own.shape[0])]
    pre = jnp.dot(block, own[...], preferred_element_type=F32)
    local_t = local_terms(seeds[...], add_pieces(pre, a, hops, pieces)).T
    local_ref[...] = local_t
    for k, out in zip(send, outs):
        put(out, chunk(k, a, local_t))


def sum_kernel(near, send, a, local_t, *refs):
    outs = refs[len(refs) - len(send) - 1 :]
    total = chunk(near, a, local_t[...])
    for other in refs[: len(refs) - len(outs)]:
        total += decode(other[...])
    put(outs[0], total)
    for k, out in zip(send, outs[1:]):
        put(out, chunk(k, a, local_t[...]))


def add_kernel(mine, *refs):
    total = mine[...]
    for other in refs[:-1]:
        total += decode(other[...])
    put(refs[-1], total)


def square_kernel(grad, last, *outs):
    me = lax.axis_index("example")
    size = outs[0].shape[0]
    for k, out in enumerate(outs):
        part = pl.ds(pl.multiple_of((me ^ k) * size, size), size)
        total = grad[part, :] + decode(last[part, :])
        out[...] = (total * total).astype(out.dtype)


def mean_kernel(scale, own, *refs):
    total = own[...]
    for other in refs[:-1]:
        total += other[...].astype(F32)
    refs[-1][...] = total * scale


def direct(activations, gate_weight, seeds):
    inputs, cotangent = activations[0], seeds[0]
    tokens, width = inputs.shape
    rows, hidden = gate_weight.shape
    count, examples = lax.axis_size("seq"), lax.axis_size("example")

    core = lax.rem(lax.axis_index("example"), 2)
    half = lax.dynamic_slice_in_dim(gate_weight, core * (rows // 2), rows // 2)
    held = {6: hop(half, "seq", 6), 2: hop(half, "seq", 2), 1: hop(half, "seq", 1)}
    held[4] = hop(lax.optimization_barrier((half, held[6]))[0], "seq", 4)
    (copied,) = call(pass_kernel, [jax.ShapeDtypeStruct(half.shape, BF16)], held[2])
    held[3] = hop(copied, "seq", 1)
    held[7] = hop(held[6], "seq", 1)
    held[5] = hop(held[4], "seq", 1)

    block = lambda dtype: jax.ShapeDtypeStruct((hidden, rows), dtype)
    late = (1, 2, 3, 6, 7, 4, 5)
    pieces = []
    for k in late:
        pieces += [held[k], hop(held[k], "example", 1)]
    six, four, local_t = call(
        functools.partial(local_kernel, late, (7, 5)),
        [block(BF16)] * 2 + [jax.ShapeDtypeStruct((hidden, tokens), BF16)],
        inputs, cotangent, gate_weight, *pieces,
    )
    six, four = hop(six, "seq", 1), hop(four, "seq", 1)
    far, two = call(functools.partial(sum_kernel, 6, (3,)), [block(BF16)] * 2, inputs, local_t, six)
    far, passed = (
        move(far, "seq", {i: 6 for i in (2, 3, 4, 5)}),
        move(far, "seq", {i: 2 for i in (0, 1, 6, 7)}),
    )
    two = hop(two, "seq", 1)
    four, none = call(
        functools.partial(sum_kernel, 4, (1,)), [block(F32), block(BF16)], inputs, local_t, four
    )
    none = hop(none, "seq", 1)
    (four,) = call(add_kernel, [block(BF16)], four, passed)
    four, far = lax.optimization_barrier((four, far))
    four = hop(four, "seq", 4)
    two = lax.optimization_barrier((two, far))[0]
    (two,) = call(functools.partial(sum_kernel, 2, ()), [block(BF16)], inputs, local_t, two, cost=1000)
    two = hop(two, "seq", 2)
    (grad,) = call(functools.partial(sum_kernel, 0, ()), [block(F32)], inputs, local_t, none, far, four)

    size = hidden // examples
    part = lambda dtype: jax.ShapeDtypeStruct((size, rows), dtype)
    own, *others = call(square_kernel, [part(F32)] + [part(BF16)] * (examples - 1), grad, two)
    others = [hop(x, "example", k + 1) for k, x in enumerate(others)]
    (total,) = call(
        functools.partial(mean_kernel, 1.0 / (tokens * count * examples)),
        (part(F32),), own, *others,
    )
    return total.T


def plain(activations, gate_weight, seeds):
    inputs, cotangent = activations[0], seeds[0]
    count, examples = lax.axis_size("seq"), lax.axis_size("example")
    weights = lax.all_gather(gate_weight, "seq", axis=0, tiled=True)
    pre = jnp.dot(inputs, weights, preferred_element_type=F32)
    local = local_terms(cotangent, pre)
    product = lax.dot_general(inputs, local, (((0,), (0,)), ((), ())), preferred_element_type=F32)
    grad = lax.psum_scatter(product, "seq", scatter_dimension=0, tiled=True)
    total = lax.psum_scatter(grad * grad, "example", scatter_dimension=1, tiled=True)
    return total * (1.0 / (inputs.shape[0] * count * examples))


def body(activations, gate_weight, seeds):
    rows, hidden = gate_weight.shape
    fits = lax.axis_size("seq") == 8 and rows % 256 == 0 and hidden % (16 * lax.axis_size("example")) == 0
    return (direct if fits else plain)(activations, gate_weight, seeds)


def solution(mesh):
    return jax.shard_map(
        body,
        mesh=mesh,
        in_specs=(P("example", "seq", None), P("seq", None), P("example", "seq", None)),
        out_specs=P("seq", "example"),
        check_vma=False,
    )
```

```python
import functools

import jax
import jax.numpy as jnp
from jax import lax
from jax.experimental import pallas as pl
from jax.experimental.pallas import tpu as pltpu
from jax.sharding import PartitionSpec as P

COST = 20_000_000_000
F32 = jnp.float32
BF16 = jnp.bfloat16


def local_terms(cotangent, pre):
    sigma = jax.nn.sigmoid(pre)
    return (cotangent.astype(F32) * sigma * (1.0 + pre * (1.0 - sigma))).astype(BF16)


def hop(x, axis, k):
    return lax.ppermute(x, axis, [(i, i ^ k) for i in range(lax.axis_size(axis))])


def move(x, axis, hops):
    return lax.ppermute(x, axis, [(i, i ^ k) for i, k in hops.items()])


def columns(block, size):
    return pl.ds(pl.multiple_of(block * size, 128), size)


def call(kernel, outs, *operands, cost=COST):
    vmem = pl.BlockSpec(memory_space=pltpu.VMEM)
    moved = sum(x.size * x.dtype.itemsize for x in (*operands, *outs))
    return pl.pallas_call(
        kernel,
        out_shape=tuple(outs),
        in_specs=[vmem] * len(operands),
        out_specs=(vmem,) * len(outs),
        compiler_params=pltpu.CompilerParams(vmem_limit_bytes=48 * 2**20),
        cost_estimate=pl.CostEstimate(flops=cost, bytes_accessed=moved, transcendentals=0),
    )(*operands)


def encode(x):
    return (x * jnp.abs(x)).astype(BF16)


def decode(y):
    y = y.astype(F32)
    root = jnp.sqrt(jnp.abs(y))
    return jnp.where(y < 0, -root, root)


def put(out, value):
    out[...] = encode(value) if out.dtype == BF16 else value


def add_pieces(pre, a, hops, pieces):
    half = pieces[0].shape[0]
    me = lax.axis_index("seq")
    core = lax.rem(lax.axis_index("example"), 2)
    for i, k in enumerate(hops):
        for flip in range(2):
            block = 2 * (me ^ k) + (core ^ flip)
            pre += jnp.dot(
                a[:, columns(block, half)], pieces[2 * i + flip][...], preferred_element_type=F32
            )
    return pre


def chunk(hops, a, local_t):
    rows = a.shape[1] // lax.axis_size("seq")
    block = lax.axis_index("seq") ^ hops
    return jnp.dot(local_t, a[:, columns(block, rows)], preferred_element_type=F32)


def pass_kernel(piece, out):
    out[...] = piece[...]


def local_kernel(hops, send, a, seeds, own, *refs):
    count = len(refs) - len(send) - 1
    pieces, outs, local_ref = refs[:count], refs[count:-1], refs[-1]
    block = a[:, columns(lax.axis_index("seq"), own.shape[0])]
    pre = jnp.dot(block, own[...], preferred_element_type=F32)
    local_t = local_terms(seeds[...], add_pieces(pre, a, hops, pieces)).T
    local_ref[...] = local_t
    for k, out in zip(send, outs):
        put(out, chunk(k, a, local_t))


def sum_kernel(near, send, a, local_t, *refs):
    outs = refs[len(refs) - len(send) - 1 :]
    total = chunk(near, a, local_t[...])
    for other in refs[: len(refs) - len(outs)]:
        total += decode(other[...])
    put(outs[0], total)
    for k, out in zip(send, outs[1:]):
        put(out, chunk(k, a, local_t[...]))


def far_kernel(far, send, a, local_t, other_a, other_t, out, next_out):
    both = jnp.dot(other_t[...], other_a[...], preferred_element_type=F32)
    put(out, both + chunk(far, a, local_t[...]))
    put(next_out, chunk(send, a, local_t[...]))


def add_kernel(mine, *refs):
    total = mine[...]
    for other in refs[:-1]:
        total += decode(other[...])
    put(refs[-1], total)


def square_kernel(grad, last, *outs):
    me = lax.axis_index("example")
    size = outs[0].shape[0]
    for k, out in enumerate(outs):
        part = pl.ds(pl.multiple_of((me ^ k) * size, size), size)
        total = grad[part, :] + decode(last[part, :])
        out[...] = (total * total).astype(out.dtype)


def mean_kernel(scale, own, *refs):
    total = own[...]
    for other in refs[:-1]:
        total += other[...].astype(F32)
    refs[-1][...] = total * scale


def direct(activations, gate_weight, seeds):
    inputs, cotangent = activations[0], seeds[0]
    tokens, width = inputs.shape
    rows, hidden = gate_weight.shape
    count, examples = lax.axis_size("seq"), lax.axis_size("example")

    core = lax.rem(lax.axis_index("example"), 2)
    half = lax.dynamic_slice_in_dim(gate_weight, core * (rows // 2), rows // 2)
    held = {6: hop(half, "seq", 6), 2: hop(half, "seq", 2), 1: hop(half, "seq", 1)}
    held[4] = hop(lax.optimization_barrier((half, held[6]))[0], "seq", 4)
    (copied,) = call(pass_kernel, [jax.ShapeDtypeStruct(half.shape, BF16)], held[2])
    held[3] = hop(copied, "seq", 1)
    held[7] = hop(held[6], "seq", 1)
    block = (lax.axis_index("seq") ^ 7) * rows
    other_a = hop(lax.dynamic_slice_in_dim(inputs, block, rows, 1), "seq", 1)
    held[5] = hop(lax.optimization_barrier((held[4], other_a))[0], "seq", 1)

    block = lambda dtype: jax.ShapeDtypeStruct((hidden, rows), dtype)
    late = (1, 2, 3, 6, 7, 4, 5)
    pieces = []
    for k in late:
        pieces += [held[k], hop(held[k], "example", 1)]
    four, local_t = call(
        functools.partial(local_kernel, late, (5,)),
        [block(BF16)] + [jax.ShapeDtypeStruct((hidden, tokens), BF16)],
        inputs, cotangent, gate_weight, *pieces,
    )
    other_t, four = hop(local_t, "seq", 1), hop(four, "seq", 1)
    far, two = call(
        functools.partial(far_kernel, 6, 3), [block(BF16)] * 2, inputs, local_t, other_a, other_t
    )
    far, passed = (
        move(far, "seq", {i: 6 for i in (2, 3, 4, 5)}),
        move(far, "seq", {i: 2 for i in (0, 1, 6, 7)}),
    )
    two = hop(two, "seq", 1)
    four, none = call(
        functools.partial(sum_kernel, 4, (1,)), [block(F32), block(BF16)], inputs, local_t, four
    )
    none = hop(none, "seq", 1)
    (four,) = call(add_kernel, [block(BF16)], four, passed)
    four = hop(four, "seq", 4)
    (two,) = call(functools.partial(sum_kernel, 2, ()), [block(BF16)], inputs, local_t, two, cost=1000)
    two = hop(two, "seq", 2)
    (grad,) = call(functools.partial(sum_kernel, 0, ()), [block(F32)], inputs, local_t, none, far, four)

    size = hidden // examples
    part = lambda dtype: jax.ShapeDtypeStruct((size, rows), dtype)
    own, *others = call(square_kernel, [part(F32)] + [part(BF16)] * (examples - 1), grad, two)
    others = [hop(x, "example", k + 1) for k, x in enumerate(others)]
    (total,) = call(
        functools.partial(mean_kernel, 1.0 / (tokens * count * examples)),
        (part(F32),), own, *others,
    )
    return total.T


def plain(activations, gate_weight, seeds):
    inputs, cotangent = activations[0], seeds[0]
    count, examples = lax.axis_size("seq"), lax.axis_size("example")
    weights = lax.all_gather(gate_weight, "seq", axis=0, tiled=True)
    pre = jnp.dot(inputs, weights, preferred_element_type=F32)
    local = local_terms(cotangent, pre)
    product = lax.dot_general(inputs, local, (((0,), (0,)), ((), ())), preferred_element_type=F32)
    grad = lax.psum_scatter(product, "seq", scatter_dimension=0, tiled=True)
    total = lax.psum_scatter(grad * grad, "example", scatter_dimension=1, tiled=True)
    return total * (1.0 / (inputs.shape[0] * count * examples))


def body(activations, gate_weight, seeds):
    rows, hidden = gate_weight.shape
    fits = lax.axis_size("seq") == 8 and rows % 256 == 0 and hidden % (16 * lax.axis_size("example")) == 0
    return (direct if fits else plain)(activations, gate_weight, seeds)


def solution(mesh):
    return jax.shard_map(
        body,
        mesh=mesh,
        in_specs=(P("example", "seq", None), P("seq", None), P("example", "seq", None)),
        out_specs=P("seq", "example"),
        check_vma=False,
    )
```

```python
import functools

import jax
import jax.numpy as jnp
from jax import lax
from jax.experimental import pallas as pl
from jax.experimental.pallas import tpu as pltpu
from jax.sharding import PartitionSpec as P

COST = 20_000_000_000
F32 = jnp.float32
BF16 = jnp.bfloat16


def local_terms(cotangent, pre):
    sigma = jax.nn.sigmoid(pre)
    return (cotangent.astype(F32) * sigma * (1.0 + pre * (1.0 - sigma))).astype(BF16)


def hop(x, axis, k):
    return lax.ppermute(x, axis, [(i, i ^ k) for i in range(lax.axis_size(axis))])


def move(x, axis, hops):
    return lax.ppermute(x, axis, [(i, i ^ k) for i, k in hops.items()])


def columns(block, size):
    return pl.ds(pl.multiple_of(block * size, 128), size)


def call(kernel, outs, *operands, cost=COST):
    vmem = pl.BlockSpec(memory_space=pltpu.VMEM)
    moved = sum(x.size * x.dtype.itemsize for x in (*operands, *outs))
    return pl.pallas_call(
        kernel,
        out_shape=tuple(outs),
        in_specs=[vmem] * len(operands),
        out_specs=(vmem,) * len(outs),
        compiler_params=pltpu.CompilerParams(vmem_limit_bytes=48 * 2**20),
        cost_estimate=pl.CostEstimate(flops=cost, bytes_accessed=moved, transcendentals=0),
    )(*operands)


def encode(x):
    return (x * jnp.abs(x)).astype(BF16)


def decode(y):
    y = y.astype(F32)
    root = jnp.sqrt(jnp.abs(y))
    return jnp.where(y < 0, -root, root)


def put(out, value):
    out[...] = encode(value) if out.dtype == BF16 else value


def add_pieces(pre, a, hops, pieces):
    half = pieces[0].shape[0]
    me = lax.axis_index("seq")
    core = lax.rem(lax.axis_index("example"), 2)
    for i, k in enumerate(hops):
        for flip in range(2):
            block = 2 * (me ^ k) + (core ^ flip)
            pre += jnp.dot(
                a[:, columns(block, half)], pieces[2 * i + flip][...], preferred_element_type=F32
            )
    return pre


def chunk(hops, a, local_t):
    rows = a.shape[1] // lax.axis_size("seq")
    block = lax.axis_index("seq") ^ hops
    return jnp.dot(local_t, a[:, columns(block, rows)], preferred_element_type=F32)


def pass_kernel(piece, out):
    out[...] = piece[...]


def local_kernel(hops, send, a, seeds, own, *refs):
    count = len(refs) - len(send) - 1
    pieces, outs, local_ref = refs[:count], refs[count:-1], refs[-1]
    block = a[:, columns(lax.axis_index("seq"), own.shape[0])]
    pre = jnp.dot(block, own[...], preferred_element_type=F32)
    local_t = local_terms(seeds[...], add_pieces(pre, a, hops, pieces)).T
    local_ref[...] = local_t
    for k, out in zip(send, outs):
        put(out, chunk(k, a, local_t))


def sum_kernel(near, send, a, local_t, *refs):
    outs = refs[len(refs) - len(send) - 1 :]
    total = chunk(near, a, local_t[...])
    for other in refs[: len(refs) - len(outs)]:
        total += decode(other[...])
    put(outs[0], total)
    for k, out in zip(send, outs[1:]):
        put(out, chunk(k, a, local_t[...]))


def far_kernel(far, send, a, local_t, other_a, other_t, out, next_out):
    both = jnp.dot(other_t[...], other_a[...], preferred_element_type=F32)
    put(out, both + chunk(far, a, local_t[...]))
    put(next_out, chunk(send, a, local_t[...]))


def add_kernel(mine, *refs):
    total = mine[...]
    for other in refs[:-1]:
        total += decode(other[...])
    put(refs[-1], total)


def square_kernel(grad, last, *outs):
    me = lax.axis_index("example")
    size = outs[0].shape[0]
    for k, out in enumerate(outs):
        part = pl.ds(pl.multiple_of((me ^ k) * size, size), size)
        total = grad[part, :] + decode(last[part, :])
        out[...] = (total * total).astype(out.dtype)


def mean_kernel(scale, own, *refs):
    total = own[...]
    for other in refs[:-1]:
        total += other[...].astype(F32)
    refs[-1][...] = total * scale


def direct(activations, gate_weight, seeds):
    inputs, cotangent = activations[0], seeds[0]
    tokens, width = inputs.shape
    rows, hidden = gate_weight.shape
    count, examples = lax.axis_size("seq"), lax.axis_size("example")

    core = lax.rem(lax.axis_index("example"), 2)
    half = lax.dynamic_slice_in_dim(gate_weight, core * (rows // 2), rows // 2)
    held = {6: hop(half, "seq", 6), 2: hop(half, "seq", 2), 1: hop(half, "seq", 1)}
    held[4] = hop(lax.optimization_barrier((half, held[6]))[0], "seq", 4)
    (copied,) = call(pass_kernel, [jax.ShapeDtypeStruct(half.shape, BF16)], held[1])
    held[3] = hop(copied, "seq", 2)
    held[7] = hop(held[6], "seq", 1)
    block = (lax.axis_index("seq") ^ 7) * rows
    other_a = hop(lax.dynamic_slice_in_dim(inputs, block, rows, 1), "seq", 1)
    held[5] = hop(lax.optimization_barrier((held[4], other_a))[0], "seq", 1)

    block = lambda dtype: jax.ShapeDtypeStruct((hidden, rows), dtype)
    late = (1, 2, 3, 6, 7, 4, 5)
    pieces = []
    for k in late:
        pieces += [held[k], hop(held[k], "example", 1)]
    four, local_t = call(
        functools.partial(local_kernel, late, (5,)),
        [block(BF16)] + [jax.ShapeDtypeStruct((hidden, tokens), BF16)],
        inputs, cotangent, gate_weight, *pieces,
    )
    other_t, four = hop(local_t, "seq", 1), hop(four, "seq", 1)
    far, two = call(
        functools.partial(far_kernel, 6, 3), [block(BF16)] * 2, inputs, local_t, other_a, other_t
    )
    far, passed = (
        move(far, "seq", {i: 6 for i in (2, 3, 4, 5)}),
        move(far, "seq", {i: 2 for i in (0, 1, 6, 7)}),
    )
    two = hop(two, "seq", 1)
    four, none = call(
        functools.partial(sum_kernel, 4, (1,)), [block(F32), block(BF16)], inputs, local_t, four
    )
    none = hop(none, "seq", 1)
    (four,) = call(add_kernel, [block(BF16)], four, passed)
    four = hop(four, "seq", 4)
    (two,) = call(functools.partial(sum_kernel, 2, ()), [block(BF16)], inputs, local_t, two, cost=1000)
    two = hop(two, "seq", 2)
    (grad,) = call(functools.partial(sum_kernel, 0, ()), [block(F32)], inputs, local_t, none, far, four)

    size = hidden // examples
    part = lambda dtype: jax.ShapeDtypeStruct((size, rows), dtype)
    own, *others = call(square_kernel, [part(F32)] + [part(BF16)] * (examples - 1), grad, two)
    others = [hop(x, "example", k + 1) for k, x in enumerate(others)]
    (total,) = call(
        functools.partial(mean_kernel, 1.0 / (tokens * count * examples)),
        (part(F32),), own, *others,
    )
    return total.T


def plain(activations, gate_weight, seeds):
    inputs, cotangent = activations[0], seeds[0]
    count, examples = lax.axis_size("seq"), lax.axis_size("example")
    weights = lax.all_gather(gate_weight, "seq", axis=0, tiled=True)
    pre = jnp.dot(inputs, weights, preferred_element_type=F32)
    local = local_terms(cotangent, pre)
    product = lax.dot_general(inputs, local, (((0,), (0,)), ((), ())), preferred_element_type=F32)
    grad = lax.psum_scatter(product, "seq", scatter_dimension=0, tiled=True)
    total = lax.psum_scatter(grad * grad, "example", scatter_dimension=1, tiled=True)
    return total * (1.0 / (inputs.shape[0] * count * examples))


def body(activations, gate_weight, seeds):
    rows, hidden = gate_weight.shape
    fits = lax.axis_size("seq") == 8 and rows % 256 == 0 and hidden % (16 * lax.axis_size("example")) == 0
    return (direct if fits else plain)(activations, gate_weight, seeds)


def solution(mesh):
    return jax.shard_map(
        body,
        mesh=mesh,
        in_specs=(P("example", "seq", None), P("seq", None), P("example", "seq", None)),
        out_specs=P("seq", "example"),
        check_vma=False,
    )
```

```python
import functools

import jax
import jax.numpy as jnp
from jax import lax
from jax.experimental import pallas as pl
from jax.experimental.pallas import tpu as pltpu
from jax.sharding import PartitionSpec as P

COST = 20_000_000_000
F32 = jnp.float32
BF16 = jnp.bfloat16


def local_terms(cotangent, pre):
    sigma = jax.nn.sigmoid(pre)
    return (cotangent.astype(F32) * sigma * (1.0 + pre * (1.0 - sigma))).astype(BF16)


def hop(x, axis, k):
    return lax.ppermute(x, axis, [(i, i ^ k) for i in range(lax.axis_size(axis))])


def move(x, axis, hops):
    return lax.ppermute(x, axis, [(i, i ^ k) for i, k in hops.items()])


def columns(block, size):
    return pl.ds(pl.multiple_of(block * size, 128), size)


def call(kernel, outs, *operands, cost=COST):
    vmem = pl.BlockSpec(memory_space=pltpu.VMEM)
    moved = sum(x.size * x.dtype.itemsize for x in (*operands, *outs))
    return pl.pallas_call(
        kernel,
        out_shape=tuple(outs),
        in_specs=[vmem] * len(operands),
        out_specs=(vmem,) * len(outs),
        compiler_params=pltpu.CompilerParams(vmem_limit_bytes=48 * 2**20),
        cost_estimate=pl.CostEstimate(flops=cost, bytes_accessed=moved, transcendentals=0),
    )(*operands)


def encode(x):
    return (x * jnp.abs(x)).astype(BF16)


def decode(y):
    y = y.astype(F32)
    root = jnp.sqrt(jnp.abs(y))
    return jnp.where(y < 0, -root, root)


def put(out, value):
    out[...] = encode(value) if out.dtype == BF16 else value


def add_pieces(pre, a, hops, pieces):
    half = pieces[0].shape[0]
    me = lax.axis_index("seq")
    core = lax.rem(lax.axis_index("example"), 2)
    x = lax.div(lax.axis_index("example"), 2)
    for i, k in enumerate(hops):
        if isinstance(k, tuple):
            k = jnp.where(x == 0, *k)
        for flip in range(2):
            block = 2 * (me ^ k) + (core ^ flip)
            pre += jnp.dot(
                a[:, columns(block, half)], pieces[2 * i + flip][...], preferred_element_type=F32
            )
    return pre


def chunk(hops, a, local_t):
    rows = a.shape[1] // lax.axis_size("seq")
    block = lax.axis_index("seq") ^ hops
    return jnp.dot(local_t, a[:, columns(block, rows)], preferred_element_type=F32)


def pass_kernel(piece, out):
    out[...] = piece[...]


def local_kernel(hops, send, a, seeds, own, *refs):
    count = len(refs) - len(send) - 1
    pieces, outs, local_ref = refs[:count], refs[count:-1], refs[-1]
    block = a[:, columns(lax.axis_index("seq"), own.shape[0])]
    pre = jnp.dot(block, own[...], preferred_element_type=F32)
    local_t = local_terms(seeds[...], add_pieces(pre, a, hops, pieces)).T
    local_ref[...] = local_t
    for k, out in zip(send, outs):
        put(out, chunk(k, a, local_t))


def sum_kernel(near, send, a, local_t, *refs):
    outs = refs[len(refs) - len(send) - 1 :]
    total = chunk(near, a, local_t[...])
    for other in refs[: len(refs) - len(outs)]:
        total += decode(other[...])
    put(outs[0], total)
    for k, out in zip(send, outs[1:]):
        put(out, chunk(k, a, local_t[...]))


def far_kernel(far, send, a, local_t, other_a, other_t, out, next_out):
    both = jnp.dot(other_t[...], other_a[...], preferred_element_type=F32)
    put(out, both + chunk(far, a, local_t[...]))
    put(next_out, chunk(send, a, local_t[...]))


def add_kernel(mine, *refs):
    total = mine[...]
    for other in refs[:-1]:
        total += decode(other[...])
    put(refs[-1], total)


def square_kernel(grad, last, *outs):
    me = lax.axis_index("example")
    size = outs[0].shape[0]
    for k, out in enumerate(outs):
        part = pl.ds(pl.multiple_of((me ^ k) * size, size), size)
        total = grad[part, :] + decode(last[part, :])
        out[...] = (total * total).astype(out.dtype)


def mean_kernel(scale, own, *refs):
    total = own[...]
    for other in refs[:-1]:
        total += other[...].astype(F32)
    refs[-1][...] = total * scale


def direct(activations, gate_weight, seeds):
    inputs, cotangent = activations[0], seeds[0]
    tokens, width = inputs.shape
    rows, hidden = gate_weight.shape
    count, examples = lax.axis_size("seq"), lax.axis_size("example")

    core = lax.rem(lax.axis_index("example"), 2)
    half = lax.dynamic_slice_in_dim(gate_weight, core * (rows // 2), rows // 2)
    everyone = ("example", "seq")
    size = examples * count
    across = [(i, i ^ (4 if i // count < 2 else 6)) for i in range(size)]
    held = {"own": lax.ppermute(half, everyone, across), 2: hop(half, "seq", 2), 1: hop(half, "seq", 1)}
    (copied,) = call(pass_kernel, [jax.ShapeDtypeStruct(half.shape, BF16)], held[1])
    held[3] = hop(copied, "seq", 2)
    block = (lax.axis_index("seq") ^ 7) * rows
    other_a = hop(lax.dynamic_slice_in_dim(inputs, block, rows, 1), "seq", 1)
    held["x"] = hop(held["own"], "example", 2)
    held["x"] = lax.optimization_barrier((held["x"], other_a))[0]
    held["y"] = hop(held["own"], "seq", 1)
    held["xy"] = hop(held["x"], "seq", 1)

    block = lambda dtype: jax.ShapeDtypeStruct((hidden, rows), dtype)
    late = (1, 2, 3, (4, 6), (6, 4), (5, 7), (7, 5))
    pieces = []
    for k in (1, 2, 3, "own", "x", "y", "xy"):
        pieces += [held[k], hop(held[k], "example", 1)]
    four, local_t = call(
        functools.partial(local_kernel, late, (5,)),
        [block(BF16)] + [jax.ShapeDtypeStruct((hidden, tokens), BF16)],
        inputs, cotangent, gate_weight, *pieces,
    )
    other_t, four = hop(local_t, "seq", 1), hop(four, "seq", 1)
    far, two = call(
        functools.partial(far_kernel, 6, 3), [block(BF16)] * 2, inputs, local_t, other_a, other_t
    )
    far, passed = (
        move(far, "seq", {i: 6 for i in (2, 3, 4, 5)}),
        move(far, "seq", {i: 2 for i in (0, 1, 6, 7)}),
    )
    two = hop(two, "seq", 1)
    four, none = call(
        functools.partial(sum_kernel, 4, (1,)), [block(F32), block(BF16)], inputs, local_t, four
    )
    none = hop(none, "seq", 1)
    (four,) = call(add_kernel, [block(BF16)], four, passed)
    four = hop(four, "seq", 4)
    (two,) = call(functools.partial(sum_kernel, 2, ()), [block(BF16)], inputs, local_t, two, cost=1000)
    two = hop(two, "seq", 2)
    (grad,) = call(functools.partial(sum_kernel, 0, ()), [block(F32)], inputs, local_t, none, far, four)

    share = hidden // examples
    part = lambda dtype: jax.ShapeDtypeStruct((share, rows), dtype)
    own, *others = call(square_kernel, [part(F32)] + [part(BF16)] * (examples - 1), grad, two)
    others = [hop(x, "example", k + 1) for k, x in enumerate(others)]
    (total,) = call(
        functools.partial(mean_kernel, 1.0 / (tokens * count * examples)),
        (part(F32),), own, *others,
    )
    return total.T


def plain(activations, gate_weight, seeds):
    inputs, cotangent = activations[0], seeds[0]
    count, examples = lax.axis_size("seq"), lax.axis_size("example")
    weights = lax.all_gather(gate_weight, "seq", axis=0, tiled=True)
    pre = jnp.dot(inputs, weights, preferred_element_type=F32)
    local = local_terms(cotangent, pre)
    product = lax.dot_general(inputs, local, (((0,), (0,)), ((), ())), preferred_element_type=F32)
    grad = lax.psum_scatter(product, "seq", scatter_dimension=0, tiled=True)
    total = lax.psum_scatter(grad * grad, "example", scatter_dimension=1, tiled=True)
    return total * (1.0 / (inputs.shape[0] * count * examples))


def body(activations, gate_weight, seeds):
    rows, hidden = gate_weight.shape
    fits = lax.axis_size("seq") == 8 and lax.axis_size("example") == 4
    fits = fits and rows % 256 == 0 and hidden % 64 == 0
    return (direct if fits else plain)(activations, gate_weight, seeds)


def solution(mesh):
    return jax.shard_map(
        body,
        mesh=mesh,
        in_specs=(P("example", "seq", None), P("seq", None), P("example", "seq", None)),
        out_specs=P("seq", "example"),
        check_vma=False,
    )
```

```python
import functools

import jax
import jax.numpy as jnp
from jax import lax
from jax.experimental import pallas as pl
from jax.experimental.pallas import tpu as pltpu
from jax.sharding import PartitionSpec as P

COST = 20_000_000_000
F32 = jnp.float32
BF16 = jnp.bfloat16


def local_terms(cotangent, pre):
    sigma = jax.nn.sigmoid(pre)
    return (cotangent.astype(F32) * sigma * (1.0 + pre * (1.0 - sigma))).astype(BF16)


def hop(x, axis, k):
    return lax.ppermute(x, axis, [(i, i ^ k) for i in range(lax.axis_size(axis))])


def move(x, axis, hops):
    return lax.ppermute(x, axis, [(i, i ^ k) for i, k in hops.items()])


def columns(block, size):
    return pl.ds(pl.multiple_of(block * size, 128), size)


def call(kernel, outs, *operands, cost=COST):
    vmem = pl.BlockSpec(memory_space=pltpu.VMEM)
    moved = sum(x.size * x.dtype.itemsize for x in (*operands, *outs))
    return pl.pallas_call(
        kernel,
        out_shape=tuple(outs),
        in_specs=[vmem] * len(operands),
        out_specs=(vmem,) * len(outs),
        compiler_params=pltpu.CompilerParams(vmem_limit_bytes=48 * 2**20),
        cost_estimate=pl.CostEstimate(flops=cost, bytes_accessed=moved, transcendentals=0),
    )(*operands)


def encode(x):
    return (x * jnp.abs(x)).astype(BF16)


def decode(y):
    y = y.astype(F32)
    root = jnp.sqrt(jnp.abs(y))
    return jnp.where(y < 0, -root, root)


def put(out, value):
    out[...] = encode(value) if out.dtype == BF16 else value


def add_pieces(pre, a, hops, pieces):
    half = pieces[0].shape[0]
    me = lax.axis_index("seq")
    core = lax.rem(lax.axis_index("example"), 2)
    x = lax.div(lax.axis_index("example"), 2)
    for i, k in enumerate(hops):
        if isinstance(k, tuple):
            k = jnp.where(x == 0, *k)
        for flip in range(2):
            block = 2 * (me ^ k) + (core ^ flip)
            pre += jnp.dot(
                a[:, columns(block, half)], pieces[2 * i + flip][...], preferred_element_type=F32
            )
    return pre


def chunk(hops, a, local_t):
    rows = a.shape[1] // lax.axis_size("seq")
    block = lax.axis_index("seq") ^ hops
    return jnp.dot(local_t, a[:, columns(block, rows)], preferred_element_type=F32)


def pass_kernel(piece, out):
    out[...] = piece[...]


def local_kernel(hops, send, a, seeds, own, *refs):
    count = len(refs) - len(send) - 1
    pieces, outs, local_ref = refs[:count], refs[count:-1], refs[-1]
    block = a[:, columns(lax.axis_index("seq"), own.shape[0])]
    pre = jnp.dot(block, own[...], preferred_element_type=F32)
    local_t = local_terms(seeds[...], add_pieces(pre, a, hops, pieces)).T
    local_ref[...] = local_t
    for k, out in zip(send, outs):
        put(out, chunk(k, a, local_t))


def sum_kernel(near, send, a, local_t, *refs):
    outs = refs[len(refs) - len(send) - 1 :]
    total = chunk(near, a, local_t[...])
    for other in refs[: len(refs) - len(outs)]:
        total += decode(other[...])
    put(outs[0], total)
    for k, out in zip(send, outs[1:]):
        put(out, chunk(k, a, local_t[...]))


def far_kernel(far, send, a, local_t, other_a, other_t, out, next_out):
    both = jnp.dot(other_t[...], other_a[...], preferred_element_type=F32)
    put(out, both + chunk(far, a, local_t[...]))
    put(next_out, chunk(send, a, local_t[...]))


def add_kernel(mine, *refs):
    total = mine[...]
    for other in refs[:-1]:
        total += decode(other[...])
    put(refs[-1], total)


def square_kernel(grad, last, *outs):
    me = lax.axis_index("example")
    size = outs[0].shape[0]
    for k, out in enumerate(outs):
        part = pl.ds(pl.multiple_of((me ^ k) * size, size), size)
        total = grad[part, :] + decode(last[part, :])
        out[...] = (total * total).astype(out.dtype)


def mean_kernel(scale, own, *refs):
    total = own[...]
    for other in refs[:-1]:
        total += other[...].astype(F32)
    refs[-1][...] = total * scale


def direct(activations, gate_weight, seeds):
    inputs, cotangent = activations[0], seeds[0]
    tokens, width = inputs.shape
    rows, hidden = gate_weight.shape
    count, examples = lax.axis_size("seq"), lax.axis_size("example")

    core = lax.rem(lax.axis_index("example"), 2)
    half = lax.dynamic_slice_in_dim(gate_weight, core * (rows // 2), rows // 2)
    everyone = ("example", "seq")
    size = examples * count
    across = [(i, i ^ (4 if i // count < 2 else 6)) for i in range(size)]
    held = {"own": lax.ppermute(half, everyone, across), 2: hop(half, "seq", 2), 1: hop(half, "seq", 1)}
    (copied,) = call(pass_kernel, [jax.ShapeDtypeStruct(half.shape, BF16)], held[1])
    held[3] = hop(copied, "seq", 2)
    block = (lax.axis_index("seq") ^ 7) * rows
    other_a = hop(lax.dynamic_slice_in_dim(inputs, block, rows, 1), "seq", 1)
    held["x"] = hop(held["own"], "example", 2)
    held["x"] = lax.optimization_barrier((held["x"], other_a))[0]
    held["y"] = hop(held["own"], "seq", 1)
    held["xy"] = hop(held["x"], "seq", 1)

    block = lambda dtype: jax.ShapeDtypeStruct((hidden, rows), dtype)
    late = (1, 2, 3, (4, 6), (6, 4), (5, 7), (7, 5))
    pieces = []
    for k in (1, 2, 3, "own", "x", "y", "xy"):
        pieces += [held[k], hop(held[k], "example", 1)]
    four, local_t = call(
        functools.partial(local_kernel, late, (5,)),
        [block(BF16)] + [jax.ShapeDtypeStruct((hidden, tokens), BF16)],
        inputs, cotangent, gate_weight, *pieces,
    )
    other_t, four = hop(local_t, "seq", 1), hop(four, "seq", 1)
    far, two = call(
        functools.partial(far_kernel, 6, 3), [block(BF16)] * 2, inputs, local_t, other_a, other_t
    )
    far, passed = (
        move(far, "seq", {i: 6 for i in (2, 3, 4, 5)}),
        move(far, "seq", {i: 2 for i in (0, 1, 6, 7)}),
    )
    two = hop(two, "seq", 1)
    four, none = call(
        functools.partial(sum_kernel, 4, (1,)), [block(F32), block(BF16)], inputs, local_t, four
    )
    none = hop(none, "seq", 1)
    (four,) = call(add_kernel, [block(BF16)], four, passed)
    four = hop(four, "seq", 4)
    (two,) = call(functools.partial(sum_kernel, 2, ()), [block(BF16)], inputs, local_t, two, cost=1000)
    two = hop(two, "seq", 2)
    (grad,) = call(functools.partial(sum_kernel, 0, ()), [block(F32)], inputs, local_t, none, far, four)

    share = hidden // examples
    part = lambda dtype: jax.ShapeDtypeStruct((share, rows), dtype)
    own, *others = call(square_kernel, [part(F32)] + [part(BF16)] * (examples - 1), grad, two)
    others = [hop(others[k - 1], "example", k) for k in (3, 2, 1)]
    (total,) = call(
        functools.partial(mean_kernel, 1.0 / (tokens * count * examples)),
        (part(F32),), own, *others,
    )
    return total.T


def plain(activations, gate_weight, seeds):
    inputs, cotangent = activations[0], seeds[0]
    count, examples = lax.axis_size("seq"), lax.axis_size("example")
    weights = lax.all_gather(gate_weight, "seq", axis=0, tiled=True)
    pre = jnp.dot(inputs, weights, preferred_element_type=F32)
    local = local_terms(cotangent, pre)
    product = lax.dot_general(inputs, local, (((0,), (0,)), ((), ())), preferred_element_type=F32)
    grad = lax.psum_scatter(product, "seq", scatter_dimension=0, tiled=True)
    total = lax.psum_scatter(grad * grad, "example", scatter_dimension=1, tiled=True)
    return total * (1.0 / (inputs.shape[0] * count * examples))


def body(activations, gate_weight, seeds):
    rows, hidden = gate_weight.shape
    fits = lax.axis_size("seq") == 8 and lax.axis_size("example") == 4
    fits = fits and rows % 256 == 0 and hidden % 64 == 0
    return (direct if fits else plain)(activations, gate_weight, seeds)


def solution(mesh):
    return jax.shard_map(
        body,
        mesh=mesh,
        in_specs=(P("example", "seq", None), P("seq", None), P("example", "seq", None)),
        out_specs=P("seq", "example"),
        check_vma=False,
    )
```
